256 devices in a mesh: blk: 8 (over y_hi, x), sec: 32 (over y_lo, z, core).
Axes of the slice: x: 4, y: 4 (y_hi: 2, y_lo: 2; y = y_hi * 2 + y_lo), z: 8, core: 2. Of those that a mesh axis runs over, the one named last changes fastest.
Arguments:
- wavefunction: float32 [16, 256, 256], P('blk', 'sec'), may hold values from -6 to 6
- sector_sizes: int32 [16, 2], replicated, may hold values from 128 to 256, as said below
- env_left: float32 [8, 32, 8, 3, 256, 256], P('blk', 'sec'), may hold values from -0.375 to 0.375
- env_right: float32 [8, 32, 8, 3, 256, 256], P('blk', 'sec'), may hold values from -0.375 to 0.375
- mpo_weight: float32 [26], replicated, may hold values from -0.4 to 0.4
- bond_index: int32 [8, 32, 8, 3], P('blk', 'sec'), may hold values from 0 to 25
- in_pair: int32 [8, 32, 8, 3], P('blk', 'sec'), may hold values from 0 to 1
- out_pair: int32 [8, 32, 8, 3], P('blk', 'sec'), may hold values from -1 to 1
Outputs:
- applied: float32 [16, 256, 256], P('blk', 'sec')
The draws below stay inside these ranges and needn't reach their ends.
Inputs may be any that keep to these rules, and one draw needn't show every extreme that they name: `sector_sizes`: row p holds the left and right states of pair p; some pair has 256 of each and another has 128 of each. `out_pair`: -1 marks an empty slot.
All inputs are finite; a program needn't handle non-finite values.
Results may differ from the reference program's by a relative error of at most 0.0001.
Values sent between devices are 32-bit elements; how exact they have to be, the bound alone decides.
No kernel may reach another device: no remote copies, remote signals or barrier semaphores. Data moves between devices by JAX's collectives and lax.ppermute only.
A program may use at most 128 MiB of HBM per device.

```python
import jax
import jax.numpy as jnp
from jax import lax

SM = 256
MINSEC = 128
W = 26
PG = 2
TPB = 3
NP = 16
N_BLK = 8
N_SEC = 32


def draw_sector_sizes(key, part):
    key = jax.random.fold_in(key, 17)
    first_key, second_key, third_key = jax.random.split(key, 3)
    counts = jax.random.randint(first_key, (NP, 2), MINSEC, SM + 1)
    largest = jax.random.randint(second_key, (), 0, NP)
    smallest = (largest + 1 + jax.random.randint(third_key, (), 0, NP - 1)) % NP
    pair_ids = jnp.arange(NP)
    counts = jnp.where((pair_ids == largest)[:, None], SM, counts)
    counts = jnp.where((pair_ids == smallest)[:, None], MINSEC, counts)
    return counts.astype(jnp.int32)


def place_ends(array, rng, low, high):
    place = [jax.random.randint(jax.random.fold_in(rng, axis), (), 0, length) for axis, length in enumerate(array.shape)]
    widest = array.shape.index(max(array.shape))
    next_to = place[:widest] + [(place[widest] + 1) % array.shape[widest]] + place[widest + 1:]
    return array.at[tuple(place)].set(low).at[tuple(next_to)].set(high)


def levels(stream_key, dims, cuts, low, top_value):
    level = 1.0
    for dim, blocks in cuts:
        heights = jax.random.uniform(jax.random.fold_in(jax.random.fold_in(stream_key, 6), dim), (blocks,), jnp.float32, low / len(cuts), top_value / len(cuts))
        level = level * jnp.repeat(jnp.exp(heights), dims[dim] // blocks).reshape((-1,) + (1,) * (len(dims) - 1 - dim))
    return level


def bell_draw(key, dims, width, limit, shards=(), held_as=jnp.bfloat16):
    values = width * jax.random.normal(key, dims, jnp.float32)
    if shards:
        values = values * levels(key, dims, shards, -0.22, 0.18)
    return jnp.clip(values, -limit, limit).astype(held_as)


def setup_inputs(seed: int = 0) -> dict:
    keys = jax.random.split(jax.random.key(seed), 9)
    wavefunction = bell_draw(keys[0], (NP, SM, SM), 1.0, 6.0, ((0, 8), (1, 32)), jnp.float32)
    sector_sizes = draw_sector_sizes(jax.random.fold_in(keys[8], 71), 0)
    env_left = bell_draw(keys[2], (N_BLK, N_SEC, N_BLK, TPB, SM, SM), SM ** -0.5, 0.375, ((0, 8), (1, 32)), jnp.float32)
    env_right = bell_draw(keys[3], (N_BLK, N_SEC, N_BLK, TPB, SM, SM), SM ** -0.5, 0.375, ((0, 8), (1, 32)), jnp.float32)
    mpo_weight = jnp.clip(jax.random.uniform(keys[4], (W,), jnp.float32, -0.4, 0.4), -0.4, 0.4)
    bond_index = place_ends(jax.random.randint(keys[5], (N_BLK, N_SEC, N_BLK, TPB), 0, W), jax.random.fold_in(keys[5], 1), 0, W - 1).astype(jnp.int32)
    in_pair = place_ends(jax.random.randint(keys[6], (N_BLK, N_SEC, N_BLK, TPB), 0, PG), jax.random.fold_in(keys[6], 1), 0, PG - 1).astype(jnp.int32)
    out_pair = place_ends(jax.random.randint(keys[7], (N_BLK, N_SEC, N_BLK, TPB), -1, PG), jax.random.fold_in(keys[7], 1), -1, PG - 1).astype(jnp.int32)
    return {"wavefunction": wavefunction, "sector_sizes": sector_sizes, "env_left": env_left, "env_right": env_right, "mpo_weight": mpo_weight, "bond_index": bond_index, "in_pair": in_pair, "out_pair": out_pair}


def reference(wavefunction, sector_sizes, env_left, env_right, mpo_weight, bond_index, in_pair, out_pair):
    states = jnp.arange(SM, dtype=jnp.int32)
    valid_mask = ((states[None, :, None] < sector_sizes[:, 0, None, None]) & (states[None, None, :] < sector_sizes[:, 1, None, None])).astype(jnp.float32)
    masked = wavefunction * valid_mask
    slot_shape = bond_index.shape
    owner_group = lax.broadcasted_iota(jnp.int32, slot_shape, 0)
    source = lax.broadcasted_iota(jnp.int32, slot_shape, 2)
    target = (owner_group * PG + jnp.maximum(out_pair, 0)).reshape(-1).astype(jnp.int32)
    anchor = (source * PG + in_pair).reshape(-1).astype(jnp.int32)
    weights = (mpo_weight[bond_index] * (out_pair >= 0).astype(jnp.float32)).reshape(-1)
    slot_count = target.shape[0]
    left_blocks = env_left.reshape(slot_count, SM, SM)
    right_blocks = env_right.reshape(slot_count, SM, SM)

    def absorb(summed, term_items):
        left_block, right_block, target_pair, anchor_pair, weight = term_items
        inner_prod = jnp.dot(left_block, masked[anchor_pair], precision=lax.Precision.HIGHEST, preferred_element_type=jnp.float32)
        term_value = jnp.dot(inner_prod, right_block.T, precision=lax.Precision.HIGHEST, preferred_element_type=jnp.float32) * weight
        return summed.at[target_pair].add(term_value), None

    summed, unused = lax.scan(absorb, jnp.zeros((NP, SM, SM), jnp.float32), (left_blocks, right_blocks, target, anchor, weights))
    return summed * valid_mask
```

```python
import functools

import jax
import jax.numpy as jnp
from jax import lax
from jax.experimental import pallas as pl
from jax.experimental.pallas import tpu as pltpu
from jax.sharding import Mesh, PartitionSpec as P

GROUPS, PAIRS, SLOTS, STATES, ROWS = 8, 2, 3, 256, 8
RUNS = STATES // (2 * ROWS)
F32, BF16 = jnp.float32, jnp.bfloat16


def split(value):
    high = value.astype(BF16)
    return high, (value - high.astype(F32)).astype(BF16)


def dot3(left, right, contract):
    dot = functools.partial(
        lax.dot_general, dimension_numbers=(contract, ((), ())), preferred_element_type=F32
    )
    return dot(left[0], right[0]) + dot(left[0], right[1]) + dot(left[1], right[0])


def contract_kernel(
    place, sizes, weight, bond, in_pair, out_pair,
    x_same, x_other, left, right, keep, give, x_high, x_low, total,
):
    step = pl.program_id(0)
    core = place[0]
    source = place[1 + step]

    @pl.when(step == 0)
    def _():
        total[...] = jnp.zeros_like(total)

    row_ids = lax.broadcasted_iota(jnp.int32, (RUNS, 2, ROWS, STATES), 0) * (2 * ROWS)
    row_ids += lax.broadcasted_iota(jnp.int32, (RUNS, 2, ROWS, STATES), 1) * ROWS
    row_ids += lax.broadcasted_iota(jnp.int32, (RUNS, 2, ROWS, STATES), 2)
    row_ids = row_ids.reshape(STATES, STATES)
    col_ids = lax.broadcasted_iota(jnp.int32, (STATES, STATES), 1)
    for pair in range(PAIRS):
        same, other = x_same[0, :, pair], x_other[0, :, pair]
        first = jnp.where(core == 0, same, other)
        second = jnp.where(core == 0, other, same)
        whole = jnp.stack([first, second], axis=1).reshape(STATES, STATES)
        here = source * PAIRS + pair
        valid = (row_ids < sizes[here, 0]) & (col_ids < sizes[here, 1])
        x_high[pair], x_low[pair] = split(jnp.where(valid, whole, 0.0))

    for slot in range(SLOTS):
        target = out_pair[source, slot]

        @pl.when(target >= 0)
        def _():
            pair = in_pair[source, slot]
            inner = dot3(split(left[0, slot]), (x_high[pair], x_low[pair]), ((1,), (0,)))
            inner = inner * weight[bond[source, slot]]
            total[target] += dot3(split(inner), split(right[0, slot]), ((1,), (1,)))

    @pl.when(step == pl.num_programs(0) - 1)
    def _():
        for pair in range(PAIRS):
            rows = total[pair].reshape(RUNS, 2, ROWS, STATES)
            keep[:, pair] = jnp.where(core == 0, rows[:, 0], rows[:, 1])
            give[:, pair] = jnp.where(core == 0, rows[:, 1], rows[:, 0])


def contract(place, sizes, weight, bond, in_pair, out_pair, x_same, x_other, left, right):
    steps = x_same.shape[0]
    panel = pl.BlockSpec((1, RUNS, PAIRS, ROWS, STATES), lambda i, *_: (i, 0, 0, 0, 0))
    env = pl.BlockSpec((1, SLOTS, STATES, STATES), lambda i, place, *_: (place[1 + i], 0, 0, 0))
    out = pl.BlockSpec((RUNS, PAIRS, ROWS, STATES), lambda i, *_: (0, 0, 0, 0))
    shape = jax.ShapeDtypeStruct((RUNS, PAIRS, ROWS, STATES), F32)
    return pl.pallas_call(
        contract_kernel,
        grid_spec=pltpu.PrefetchScalarGridSpec(
            num_scalar_prefetch=6,
            grid=(steps,),
            in_specs=[panel, panel, env, env],
            out_specs=[out, out],
            scratch_shapes=[
                pltpu.VMEM((PAIRS, STATES, STATES), BF16),
                pltpu.VMEM((PAIRS, STATES, STATES), BF16),
                pltpu.VMEM((PAIRS, STATES, STATES), F32),
            ],
        ),
        out_shape=[shape, shape],
        compiler_params=pltpu.CompilerParams(vmem_limit_bytes=32 * 2**20),
    )(place, sizes, weight, bond, in_pair, out_pair, x_same, x_other, left, right)


def swap_core(value):
    return lax.ppermute(value, "core", [(0, 1), (1, 0)])


def local(
    wavefunction, sector_sizes, env_left, env_right, mpo_weight, bond_index, in_pair, out_pair
):
    core = lax.axis_index("core")
    my_y, my_x = lax.axis_index("y_hi"), lax.axis_index("x")
    runs = lax.all_to_all(
        jnp.broadcast_to(wavefunction[None], (RUNS,) + wavefunction.shape), ("y_lo", "z"), 0, 0
    )
    across = lax.ppermute(runs, "y_hi", [(0, 1), (1, 0)])
    pieces, sources = [runs, across], [my_y * 4 + my_x, (1 - my_y) * 4 + my_x]
    for step in (1, 3, 2):
        ring = [(x, (x + step) % 4) for x in range(4)]
        there = (my_x - step) % 4
        pieces += [lax.ppermute(runs, "x", ring), lax.ppermute(across, "x", ring)]
        sources += [my_y * 4 + there, (1 - my_y) * 4 + there]
    x_same = jnp.stack(pieces)
    x_other = swap_core(x_same)
    place = jnp.stack([core] + sources).astype(jnp.int32)
    keep, give = contract(
        place, sector_sizes, mpo_weight, bond_index[0, 0], in_pair[0, 0], out_pair[0, 0],
        x_same, x_other, env_left[0, 0], env_right[0, 0],
    )
    half = keep + swap_core(give)
    summed = lax.all_to_all(half, ("y_lo", "z"), 0, 0).sum(0)

    owner = (lax.axis_index("y_lo") * 8 + lax.axis_index("z")) * 2 + core
    group_sizes = lax.dynamic_slice_in_dim(
        sector_sizes, (my_y * 4 + my_x) * PAIRS, PAIRS, 0
    )
    row_ids = owner * ROWS + jnp.arange(ROWS, dtype=jnp.int32)
    col_ids = jnp.arange(STATES, dtype=jnp.int32)
    valid = (row_ids[None, :, None] < group_sizes[:, 0, None, None]) & (
        col_ids[None, None, :] < group_sizes[:, 1, None, None]
    )
    return jnp.where(valid, summed, 0.0)


def solution(mesh):
    fine = Mesh(mesh.devices.reshape(2, 4, 2, 8, 2), ("y_hi", "x", "y_lo", "z", "core"))
    blk, sec = ("y_hi", "x"), ("y_lo", "z", "core")
    return jax.shard_map(
        local,
        mesh=fine,
        in_specs=(
            P(blk, sec, None),
            P(),
            P(blk, sec, None, None, None, None),
            P(blk, sec, None, None, None, None),
            P(),
            P(blk, sec, None, None),
            P(blk, sec, None, None),
            P(blk, sec, None, None),
        ),
        out_specs=P(blk, sec, None),
        check_vma=False,
    )
```

```python
import functools

import jax
import jax.numpy as jnp
from jax import lax
from jax.experimental import pallas as pl
from jax.experimental.pallas import tpu as pltpu
from jax.sharding import Mesh, PartitionSpec as P

GROUPS, PAIRS, SLOTS, STATES, ROWS = 8, 2, 3, 256, 8
RUNS = STATES // (2 * ROWS)
F32, BF16 = jnp.float32, jnp.bfloat16
SUMS = (PAIRS, STATES, STATES)
AHEAD = 1
STEPS = (0, 1, 3, 2)
LIMIT = 48 * 2**20
LONG = 20 * 10**9
HALF = (RUNS, PAIRS, ROWS, STATES)


def split(value):
    high = value.astype(BF16)
    return high, (value - high.astype(F32)).astype(BF16)


def dot3(left, right, contract):
    dot = functools.partial(
        lax.dot_general, dimension_numbers=(contract, ((), ())), preferred_element_type=F32
    )
    return dot(left[0], right[0]) + dot(left[0], right[1]) + dot(left[1], right[0])


def interleave(even, odd):
    return jnp.stack([even, odd], axis=1).reshape(STATES, STATES)


def chunk_kernel(parts, sizes, codes, scales, *refs):
    panels, refs = refs[: 4 * parts], refs[4 * parts :]
    left, right, keep, give, total, x_high, x_low, lefts, rights, done = refs
    core, my_y, my_x = lax.axis_index("core"), lax.axis_index("y_hi"), lax.axis_index("x")
    sources = [
        y * 4 + lax.rem(my_x + 4 - step, 4) for y in (my_y, 1 - my_y) for step in STEPS
    ]

    def env(j):
        source = sources[j]
        return (
            pltpu.make_async_copy(left.at[source], lefts.at[j], done.at[j, 0]),
            pltpu.make_async_copy(right.at[source], rights.at[j], done.at[j, 1]),
        )

    def fetch(j):
        for copy in env(j):
            copy.start()

    row_ids = lax.broadcasted_iota(jnp.int32, (STATES, STATES), 0)
    col_ids = lax.broadcasted_iota(jnp.int32, (STATES, STATES), 1)

    def rows(j):
        for pair in range(PAIRS):
            (same, at), (other, _) = panels[4 * j + 2 * pair : 4 * j + 2 * pair + 2]
            same, other = same[at], other[at]
            even = jnp.where(core == 0, same, other)
            odd = jnp.where(core == 0, other, same)
            here = sources[j] * PAIRS + pair
            valid = (row_ids < sizes[0, here]) & (col_ids < sizes[1, here])
            whole = jnp.where(valid, interleave(even, odd), 0.0)
            x_high[j % 2, pair], x_low[j % 2, pair] = split(whole)

    def products(j):
        inner = []
        for slot in range(SLOTS):
            pair = codes[0, slot, 0, sources[j]] // 2
            x = x_high[j % 2, pair], x_low[j % 2, pair]
            product = dot3(split(lefts[j, slot]), x, ((1,), (0,)))
            inner.append(split(product * scales[0, slot, 0, sources[j]]))
        return inner

    def add(j, inner):
        for slot in range(SLOTS):
            total[codes[0, slot, 0, sources[j]] % 2] += dot3(inner[slot], split(rights[j, slot]), ((1,), (1,)))

    for j in range(AHEAD):
        fetch(j)
    total[...] = jnp.zeros(SUMS, F32)
    rows(0)
    inner = None
    for j in range(parts + 1):
        if j + AHEAD < parts:
            fetch(j + AHEAD)
        if j < parts:
            env(j)[0].wait()
        if j > 0:
            env(j - 1)[1].wait()
        coming = products(j) if j < parts else None
        if j + 1 < parts:
            rows(j + 1)
        if j > 0:
            add(j - 1, inner)
        inner = coming
    for pair in range(PAIRS):
        pairs = total[pair].reshape(RUNS, 2, ROWS, STATES)
        keep[:, pair] = jnp.where(core == 0, pairs[:, 0], pairs[:, 1])
        give[:, pair] = jnp.where(core == 0, pairs[:, 1], pairs[:, 0])


def chunk(lists, panels, left, right, estimate):
    parts = len(panels) // 4
    smem, vmem, hbm = (
        pl.BlockSpec(memory_space=space)
        for space in (pltpu.SMEM, pltpu.VMEM, pl.ANY)
    )
    arrays = []
    for array, _ in panels:
        if not any(array is known for known in arrays):
            arrays.append(array)
    at = [[array is known for known in arrays].index(True) for array, _ in panels]

    def kernel(*refs):
        here = [(refs[3 + k], index) for k, (_, index) in zip(at, panels)]
        chunk_kernel(parts, *refs[:3], *here, *refs[3 + len(arrays) :])

    return pl.pallas_call(
        kernel,
        in_specs=[smem] * 3 + [vmem] * len(arrays) + [hbm] * 2,
        out_specs=[vmem] * 2,
        out_shape=[jax.ShapeDtypeStruct(HALF, F32)] * 2,
        scratch_shapes=[
            pltpu.VMEM(SUMS, F32),
            pltpu.VMEM((2,) + SUMS, BF16),
            pltpu.VMEM((2,) + SUMS, BF16),
            pltpu.VMEM((parts, SLOTS, STATES, STATES), F32),
            pltpu.VMEM((parts, SLOTS, STATES, STATES), F32),
            pltpu.SemaphoreType.DMA((parts, 2)),
        ],
        cost_estimate=pl.CostEstimate(flops=estimate, bytes_accessed=2**20, transcendentals=0),
        compiler_params=pltpu.CompilerParams(vmem_limit_bytes=LIMIT),
    )(*lists, *arrays, left, right)


def swap_core(value):
    return lax.ppermute(value, "core", [(0, 1), (1, 0)])


def ahead(value, step):
    return lax.ppermute(value, "x", [(x, (x + step) % 4) for x in range(4)])


def across(value):
    return lax.ppermute(value, "y_hi", [(0, 1), (1, 0)])


def local(
    wavefunction, sector_sizes, env_left, env_right, mpo_weight, bond_index, in_pair, out_pair
):
    core = lax.axis_index("core")
    my_y, my_x = lax.axis_index("y_hi"), lax.axis_index("x")
    left, right = env_left[0, 0], env_right[0, 0]

    runs = lax.all_to_all(
        jnp.broadcast_to(wavefunction[None], (RUNS,) + wavefunction.shape), ("y_lo", "z"), 0, 0
    )
    first, second = runs[None, :, 0], runs[None, :, 1]
    live = out_pair >= 0
    picked = bond_index[..., None] == jnp.arange(mpo_weight.shape[0], dtype=jnp.int32)
    scales = jnp.where(live, jnp.sum(jnp.where(picked, mpo_weight, 0.0), axis=-1), 0.0)
    codes = in_pair * 2 + jnp.maximum(out_pair, 0)
    lists = (
        jnp.minimum(sector_sizes.T, STATES),
        *[lax.transpose(array, (0, 3, 1, 2)) for array in (codes, scales)],
    )
    (crossed, *beside), lists = lax.optimization_barrier(
        ([across(first), *[ahead(second, step) for step in STEPS[1:]]], lists)
    )
    column = jnp.concatenate([first, crossed])
    row = jnp.concatenate([second, *beside])
    far_row = across(row)
    columns = [column] + [ahead(column, step) for step in STEPS[1:]]

    mid = jnp.concatenate(columns[1:])
    both = [(column, swap_core(column), 0)] + [(mid, swap_core(mid), 2 * k) for k in range(3)]
    panels = []
    for side, here in enumerate((row, far_row)):
        other = swap_core(here)
        for k in range(4):
            panels += [(array, both[k][2] + side) for array in both[k][:2]] + [(here, k), (other, k)]
    keep, give = chunk(lists, panels, left, right, LONG)
    half = keep + swap_core(give)
    summed = lax.all_to_all(half, ("y_lo", "z"), 0, 0).sum(0)

    owner = (lax.axis_index("y_lo") * 8 + lax.axis_index("z")) * 2 + core
    group_sizes = lax.dynamic_slice_in_dim(sector_sizes, (my_y * 4 + my_x) * PAIRS, PAIRS, 0)
    row_ids = owner * ROWS + jnp.arange(ROWS, dtype=jnp.int32)
    col_ids = jnp.arange(STATES, dtype=jnp.int32)
    valid = (row_ids[None, :, None] < group_sizes[:, 0, None, None]) & (
        col_ids[None, None, :] < group_sizes[:, 1, None, None]
    )
    return jnp.where(valid, summed, 0.0)


def solution(mesh):
    fine = Mesh(mesh.devices.reshape(2, 4, 2, 8, 2), ("y_hi", "x", "y_lo", "z", "core"))
    blk, sec = ("y_hi", "x"), ("y_lo", "z", "core")
    return jax.shard_map(
        local,
        mesh=fine,
        in_specs=(
            P(blk, sec, None),
            P(),
            P(blk, sec, None, None, None, None),
            P(blk, sec, None, None, None, None),
            P(),
            P(blk, sec, None, None),
            P(blk, sec, None, None),
            P(blk, sec, None, None),
        ),
        out_specs=P(blk, sec, None),
        check_vma=False,
    )
```

```python
import functools

import jax
import jax.numpy as jnp
from jax import lax
from jax.experimental import pallas as pl
from jax.experimental.pallas import tpu as pltpu
from jax.sharding import Mesh, PartitionSpec as P

GROUPS, PAIRS, SLOTS, STATES, ROWS = 8, 2, 3, 256, 8
RUNS = STATES // (2 * ROWS)
F32, BF16 = jnp.float32, jnp.bfloat16
SUMS = (PAIRS, STATES, STATES)
AHEAD = 2
STEPS = (0, 1, 3, 2)
LIMIT = 48 * 2**20
LONG = 20 * 10**9
HALF = (RUNS, PAIRS, ROWS, STATES)


def split(value):
    high = value.astype(BF16)
    return high, (value - high.astype(F32)).astype(BF16)


def dot3(left, right, contract):
    dot = functools.partial(
        lax.dot_general, dimension_numbers=(contract, ((), ())), preferred_element_type=F32
    )
    return dot(left[0], right[0]) + dot(left[0], right[1]) + dot(left[1], right[0])


def interleave(even, odd):
    return jnp.stack([even, odd], axis=1).reshape(STATES, STATES)


def chunk_kernel(parts, last, sizes, codes, scales, *refs):
    panels, refs = refs[: 4 * len(parts)], refs[4 * len(parts) :]
    left, right, *refs = refs
    if last:
        before, keep, give, total, *refs = refs
    else:
        total, *refs = refs
    x_high, x_low, lefts, rights, done = refs
    core, my_y, my_x = lax.axis_index("core"), lax.axis_index("y_hi"), lax.axis_index("x")
    sources = [
        (my_y, 1 - my_y)[side] * 4 + lax.rem(my_x + 4 - STEPS[k], 4) for side, k in parts
    ]

    def env(j):
        source = sources[j]
        return (
            pltpu.make_async_copy(left.at[source], lefts.at[j], done.at[j, 0]),
            pltpu.make_async_copy(right.at[source], rights.at[j], done.at[j, 1]),
        )

    def fetch(j):
        for copy in env(j):
            copy.start()

    row_ids = lax.broadcasted_iota(jnp.int32, (STATES, STATES), 0)
    col_ids = lax.broadcasted_iota(jnp.int32, (STATES, STATES), 1)

    def rows(j):
        for pair in range(PAIRS):
            same, other = [
                ref[at, :, pair] if whole else ref[at]
                for ref, at, whole in panels[4 * j + 2 * pair : 4 * j + 2 * pair + 2]
            ]
            even = jnp.where(core == 0, same, other)
            odd = jnp.where(core == 0, other, same)
            here = sources[j] * PAIRS + pair
            valid = (row_ids < sizes[0, here]) & (col_ids < sizes[1, here])
            x_high[j, pair], x_low[j, pair] = split(jnp.where(valid, interleave(even, odd), 0.0))

    for j in range(AHEAD):
        fetch(j)
    total[...] = before[...] if last else jnp.zeros(SUMS, F32)
    for j in range(len(parts)):
        rows(j)
    for j, source in enumerate(sources):
        if j + AHEAD < len(parts):
            fetch(j + AHEAD)
        for copy in env(j):
            copy.wait()
        inner = []
        for slot in range(SLOTS):
            pair = codes[0, slot, 0, source] // 2
            x = x_high[j, pair], x_low[j, pair]
            product = dot3(split(lefts[j, slot]), x, ((1,), (0,)))
            inner.append(split(product * scales[0, slot, 0, source]))
        for slot in range(SLOTS):
            target = codes[0, slot, 0, source] % 2
            total[target] += dot3(inner[slot], split(rights[j, slot]), ((1,), (1,)))
    if last:
        for pair in range(PAIRS):
            pairs = total[pair].reshape(RUNS, 2, ROWS, STATES)
            keep[:, pair] = jnp.where(core == 0, pairs[:, 0], pairs[:, 1])
            give[:, pair] = jnp.where(core == 0, pairs[:, 1], pairs[:, 0])


def chunk(parts, lists, panels, left, right, before):
    last = before is not None
    count = len(parts)
    smem, vmem, hbm = (
        pl.BlockSpec(memory_space=space) for space in (pltpu.SMEM, pltpu.VMEM, pl.ANY)
    )
    arrays = []
    for array, *_ in panels:
        if not any(array is known for known in arrays):
            arrays.append(array)
    at = [[array is known for known in arrays].index(True) for array, *_ in panels]

    def kernel(*refs):
        here = [(refs[3 + k], *panel[1:]) for k, panel in zip(at, panels)]
        chunk_kernel(parts, last, *refs[:3], *here, *refs[3 + len(arrays) :])

    result = pl.pallas_call(
        kernel,
        in_specs=[smem] * 3 + [vmem] * len(arrays) + [hbm] * 2 + [vmem] * last,
        out_specs=[vmem] * (2 if last else 1),
        out_shape=[jax.ShapeDtypeStruct(HALF, F32)] * 2
        if last
        else [jax.ShapeDtypeStruct(SUMS, F32)],
        scratch_shapes=[pltpu.VMEM(SUMS, F32)] * last
        + [
            pltpu.VMEM((count,) + SUMS, BF16),
            pltpu.VMEM((count,) + SUMS, BF16),
            pltpu.VMEM((count, SLOTS, STATES, STATES), F32),
            pltpu.VMEM((count, SLOTS, STATES, STATES), F32),
            pltpu.SemaphoreType.DMA((count, 2)),
        ],
        cost_estimate=pl.CostEstimate(flops=LONG if last else 10**9, bytes_accessed=2**20, transcendentals=0),
        compiler_params=pltpu.CompilerParams(vmem_limit_bytes=LIMIT),
    )(*lists, *arrays, left, right, *([before] if last else []))
    return result if last else result[0]


def swap_core(value):
    return lax.ppermute(value, "core", [(0, 1), (1, 0)])


def ahead(value, step):
    return lax.ppermute(value, "x", [(x, (x + step) % 4) for x in range(4)])


def across(value):
    return lax.ppermute(value, "y_hi", [(0, 1), (1, 0)])


def local(
    wavefunction, sector_sizes, env_left, env_right, mpo_weight, bond_index, in_pair, out_pair
):
    core = lax.axis_index("core")
    my_y, my_x = lax.axis_index("y_hi"), lax.axis_index("x")
    left, right = env_left[0, 0], env_right[0, 0]

    runs = lax.all_to_all(
        jnp.broadcast_to(wavefunction[None], (RUNS,) + wavefunction.shape), ("y_lo", "z"), 0, 0
    )
    runs = runs[None]
    live = out_pair >= 0
    picked = bond_index[..., None] == jnp.arange(mpo_weight.shape[0], dtype=jnp.int32)
    scales = jnp.where(live, jnp.sum(jnp.where(picked, mpo_weight, 0.0), axis=-1), 0.0)
    codes = in_pair * 2 + jnp.maximum(out_pair, 0)
    lists = (
        jnp.minimum(sector_sizes.T, STATES),
        *[lax.transpose(array, (0, 3, 1, 2)) for array in (codes, scales)],
    )
    (crossed, *beside), lists = lax.optimization_barrier(
        ([across(runs), *[ahead(runs, step) for step in STEPS[1:]]], lists)
    )
    near = jnp.concatenate([runs, *beside])
    far_first = [ahead(crossed[:, :, 0], step) for step in STEPS[1:]]
    far_second = across(near[1:, :, 1])

    near_other, crossed_other = swap_core(near), swap_core(crossed)
    parts = [(0, 0), (1, 0), (0, 1), (0, 2), (0, 3)]
    panels = []
    for side, k in parts:
        both = (near, near_other) if side == 0 else (crossed, crossed_other)
        panels += [(array, k, True) for array in both] * 2
    sums = chunk(parts, lists, panels, left, right, None)

    far_first, far_second, sums = lax.optimization_barrier((far_first, far_second, sums))
    far_first = jnp.concatenate(far_first)
    far = (far_first, swap_core(far_first), far_second, swap_core(far_second))
    parts = [(1, 1), (1, 2), (1, 3)]
    panels = [(array, k - 1, False) for _, k in parts for array in far]
    keep, give = chunk(parts, lists, panels, left, right, sums)
    half = keep + swap_core(give)
    summed = lax.all_to_all(half, ("y_lo", "z"), 0, 0).sum(0)

    owner = (lax.axis_index("y_lo") * 8 + lax.axis_index("z")) * 2 + core
    group_sizes = lax.dynamic_slice_in_dim(sector_sizes, (my_y * 4 + my_x) * PAIRS, PAIRS, 0)
    row_ids = owner * ROWS + jnp.arange(ROWS, dtype=jnp.int32)
    col_ids = jnp.arange(STATES, dtype=jnp.int32)
    valid = (row_ids[None, :, None] < group_sizes[:, 0, None, None]) & (
        col_ids[None, None, :] < group_sizes[:, 1, None, None]
    )
    return jnp.where(valid, summed, 0.0)


def solution(mesh):
    fine = Mesh(mesh.devices.reshape(2, 4, 2, 8, 2), ("y_hi", "x", "y_lo", "z", "core"))
    blk, sec = ("y_hi", "x"), ("y_lo", "z", "core")
    return jax.shard_map(
        local,
        mesh=fine,
        in_specs=(
            P(blk, sec, None),
            P(),
            P(blk, sec, None, None, None, None),
            P(blk, sec, None, None, None, None),
            P(),
            P(blk, sec, None, None),
            P(blk, sec, None, None),
            P(blk, sec, None, None),
        ),
        out_specs=P(blk, sec, None),
        check_vma=False,
    )
```

```python
import functools

import jax
import jax.numpy as jnp
from jax import lax
from jax.experimental import pallas as pl
from jax.experimental.pallas import tpu as pltpu
from jax.sharding import Mesh, PartitionSpec as P

GROUPS, PAIRS, SLOTS, STATES, ROWS = 8, 2, 3, 256, 8
RUNS = STATES // (2 * ROWS)
F32, BF16 = jnp.float32, jnp.bfloat16
SUMS = (PAIRS, STATES, STATES)
AHEAD = 2
STEPS = (0, 1, 3, 2)
LIMIT = 48 * 2**20
LONG = 20 * 10**9
HALF = (RUNS, PAIRS, ROWS, STATES)


def split(value):
    high = value.astype(BF16)
    return high, (value - high.astype(F32)).astype(BF16)


def dot3(left, right, contract):
    dot = functools.partial(
        lax.dot_general, dimension_numbers=(contract, ((), ())), preferred_element_type=F32
    )
    return dot(left[0], right[0]) + dot(left[0], right[1]) + dot(left[1], right[0])


def interleave(even, odd):
    return jnp.stack([even, odd], axis=1).reshape(STATES, STATES)


def chunk_kernel(parts, last, sizes, codes, scales, *refs):
    panels, refs = refs[: 4 * len(parts)], refs[4 * len(parts) :]
    left, right, *refs = refs
    if last:
        before, keep, give, total, *refs = refs
    else:
        total, *refs = refs
    x_high, x_low, lefts, rights, done = refs
    core, my_y, my_x = lax.axis_index("core"), lax.axis_index("y_hi"), lax.axis_index("x")
    sources = [
        (my_y, 1 - my_y)[side] * 4 + lax.rem(my_x + 4 - STEPS[k], 4) for side, k in parts
    ]

    def env(j):
        source = sources[j]
        return (
            pltpu.make_async_copy(left.at[source], lefts.at[j], done.at[j, 0]),
            pltpu.make_async_copy(right.at[source], rights.at[j], done.at[j, 1]),
        )

    def fetch(j):
        for copy in env(j):
            copy.start()

    row_ids = lax.broadcasted_iota(jnp.int32, (STATES, STATES), 0)
    col_ids = lax.broadcasted_iota(jnp.int32, (STATES, STATES), 1)

    def rows(j):
        for pair in range(PAIRS):
            same, other = [
                ref[at, :, pair] if whole else ref[at]
                for ref, at, whole in panels[4 * j + 2 * pair : 4 * j + 2 * pair + 2]
            ]
            even = jnp.where(core == 0, same, other)
            odd = jnp.where(core == 0, other, same)
            here = sources[j] * PAIRS + pair
            valid = (row_ids < sizes[0, here]) & (col_ids < sizes[1, here])
            x_high[j, pair], x_low[j, pair] = split(jnp.where(valid, interleave(even, odd), 0.0))

    for j in range(AHEAD):
        fetch(j)
    total[...] = before[...] if last else jnp.zeros(SUMS, F32)
    for j in range(len(parts)):
        rows(j)
    for j, source in enumerate(sources):
        if j + AHEAD < len(parts):
            fetch(j + AHEAD)
        for copy in env(j):
            copy.wait()
        inner = []
        for slot in range(SLOTS):
            pair = codes[0, slot, 0, source] // 2
            x = x_high[j, pair], x_low[j, pair]
            product = dot3(split(lefts[j, slot]), x, ((1,), (0,)))
            inner.append(split(product * scales[0, slot, 0, source]))
        for slot in range(SLOTS):
            target = codes[0, slot, 0, source] % 2
            total[target] += dot3(inner[slot], split(rights[j, slot]), ((1,), (1,)))
    if last:
        for pair in range(PAIRS):
            pairs = total[pair].reshape(RUNS, 2, ROWS, STATES)
            keep[:, pair] = jnp.where(core == 0, pairs[:, 0], pairs[:, 1])
            give[:, pair] = jnp.where(core == 0, pairs[:, 1], pairs[:, 0])


def chunk(parts, lists, panels, left, right, before):
    last = before is not None
    count = len(parts)
    smem, vmem, hbm = (
        pl.BlockSpec(memory_space=space) for space in (pltpu.SMEM, pltpu.VMEM, pl.ANY)
    )
    arrays = []
    for array, *_ in panels:
        if not any(array is known for known in arrays):
            arrays.append(array)
    at = [[array is known for known in arrays].index(True) for array, *_ in panels]

    def kernel(*refs):
        here = [(refs[3 + k], *panel[1:]) for k, panel in zip(at, panels)]
        chunk_kernel(parts, last, *refs[:3], *here, *refs[3 + len(arrays) :])

    result = pl.pallas_call(
        kernel,
        in_specs=[smem] * 3 + [vmem] * len(arrays) + [hbm] * 2 + [vmem] * last,
        out_specs=[vmem] * (2 if last else 1),
        out_shape=[jax.ShapeDtypeStruct(HALF, F32)] * 2
        if last
        else [jax.ShapeDtypeStruct(SUMS, F32)],
        scratch_shapes=[pltpu.VMEM(SUMS, F32)] * last
        + [
            pltpu.VMEM((count,) + SUMS, BF16),
            pltpu.VMEM((count,) + SUMS, BF16),
            pltpu.VMEM((count, SLOTS, STATES, STATES), F32),
            pltpu.VMEM((count, SLOTS, STATES, STATES), F32),
            pltpu.SemaphoreType.DMA((count, 2)),
        ],
        cost_estimate=pl.CostEstimate(flops=LONG if last else 10**9, bytes_accessed=2**20, transcendentals=0),
        compiler_params=pltpu.CompilerParams(vmem_limit_bytes=LIMIT),
    )(*lists, *arrays, left, right, *([before] if last else []))
    return result if last else result[0]


def swap_core(value):
    return lax.ppermute(value, "core", [(0, 1), (1, 0)])


def ahead(value, step):
    return lax.ppermute(value, "x", [(x, (x + step) % 4) for x in range(4)])


def across(value):
    return lax.ppermute(value, "y_hi", [(0, 1), (1, 0)])


def local(
    wavefunction, sector_sizes, env_left, env_right, mpo_weight, bond_index, in_pair, out_pair
):
    core = lax.axis_index("core")
    my_y, my_x = lax.axis_index("y_hi"), lax.axis_index("x")
    left, right = env_left[0, 0], env_right[0, 0]

    runs = lax.all_to_all(
        jnp.broadcast_to(wavefunction[None], (RUNS,) + wavefunction.shape), ("y_lo", "z"), 0, 0
    )
    runs = runs[None]
    live = out_pair >= 0
    picked = bond_index[..., None] == jnp.arange(mpo_weight.shape[0], dtype=jnp.int32)
    scales = jnp.where(live, jnp.sum(jnp.where(picked, mpo_weight, 0.0), axis=-1), 0.0)
    codes = in_pair * 2 + jnp.maximum(out_pair, 0)
    lists = (
        jnp.minimum(sector_sizes.T, STATES),
        *[lax.transpose(array, (0, 3, 1, 2)) for array in (codes, scales)],
    )
    (crossed, *beside), lists = lax.optimization_barrier(
        ([across(runs), *[ahead(runs, step) for step in STEPS[1:3]]], lists)
    )
    column, row = jnp.concatenate([runs, crossed]), jnp.concatenate(beside)
    far_row, far_column = across(row), ahead(column, STEPS[3])

    near = [runs, crossed, *beside]
    panels = []
    for piece in near:
        other = swap_core(piece)
        panels += [(array, 0, True) for array in (piece, other)] * 2
    sums = chunk([(0, 0), (1, 0), (0, 1), (0, 2)], lists, panels, left, right, None)

    far_row, far_column, sums = lax.optimization_barrier((far_row, far_column, sums))
    row, column = (far_row, swap_core(far_row)), (far_column, swap_core(far_column))
    places = [(row, 0), (row, 1), (column, 0), (column, 1)]
    panels = [(array, at, True) for held, at in places for array in held * 2]
    parts = [(1, 1), (1, 2), (0, 3), (1, 3)]
    keep, give = chunk(parts, lists, panels, left, right, sums)
    half = keep + swap_core(give)
    summed = lax.all_to_all(half, ("y_lo", "z"), 0, 0).sum(0)

    owner = (lax.axis_index("y_lo") * 8 + lax.axis_index("z")) * 2 + core
    group_sizes = lax.dynamic_slice_in_dim(sector_sizes, (my_y * 4 + my_x) * PAIRS, PAIRS, 0)
    row_ids = owner * ROWS + jnp.arange(ROWS, dtype=jnp.int32)
    col_ids = jnp.arange(STATES, dtype=jnp.int32)
    valid = (row_ids[None, :, None] < group_sizes[:, 0, None, None]) & (
        col_ids[None, None, :] < group_sizes[:, 1, None, None]
    )
    return jnp.where(valid, summed, 0.0)


def solution(mesh):
    fine = Mesh(mesh.devices.reshape(2, 4, 2, 8, 2), ("y_hi", "x", "y_lo", "z", "core"))
    blk, sec = ("y_hi", "x"), ("y_lo", "z", "core")
    return jax.shard_map(
        local,
        mesh=fine,
        in_specs=(
            P(blk, sec, None),
            P(),
            P(blk, sec, None, None, None, None),
            P(blk, sec, None, None, None, None),
            P(),
            P(blk, sec, None, None),
            P(blk, sec, None, None),
            P(blk, sec, None, None),
        ),
        out_specs=P(blk, sec, None),
        check_vma=False,
    )
```

```python
import functools

import jax
import jax.numpy as jnp
from jax import lax
from jax.experimental import pallas as pl
from jax.experimental.pallas import tpu as pltpu
from jax.sharding import Mesh, PartitionSpec as P

GROUPS, PAIRS, SLOTS, STATES, ROWS = 8, 2, 3, 256, 8
RUNS = STATES // (2 * ROWS)
F32, BF16 = jnp.float32, jnp.bfloat16
SUMS = (PAIRS, STATES, STATES)
AHEAD = 2
STEPS = (0, 1, 3, 2)
LIMIT = 48 * 2**20
LONG = 20 * 10**9
HALF = (RUNS, PAIRS, ROWS, STATES)


def split(value):
    high = value.astype(BF16)
    return high, (value - high.astype(F32)).astype(BF16)


def dot3(left, right, contract):
    dot = functools.partial(
        lax.dot_general, dimension_numbers=(contract, ((), ())), preferred_element_type=F32
    )
    return dot(left[0], right[0]) + dot(left[0], right[1]) + dot(left[1], right[0])


def interleave(even, odd):
    return jnp.stack([even, odd], axis=1).reshape(STATES, STATES)


def chunk_kernel(parts, last, sizes, codes, scales, *refs):
    panels, refs = refs[: 4 * len(parts)], refs[4 * len(parts) :]
    left, right, *refs = refs
    if last:
        before, keep, give, total, *refs = refs
    else:
        total, *refs = refs
    x_high, x_low, lefts, rights, done = refs
    core, my_y, my_x = lax.axis_index("core"), lax.axis_index("y_hi"), lax.axis_index("x")
    sources = [
        (my_y, 1 - my_y)[side] * 4 + lax.rem(my_x + 4 - STEPS[k], 4) for side, k in parts
    ]

    def env(j):
        source = sources[j]
        return (
            pltpu.make_async_copy(left.at[source], lefts.at[j], done.at[j, 0]),
            pltpu.make_async_copy(right.at[source], rights.at[j], done.at[j, 1]),
        )

    def fetch(j):
        for copy in env(j):
            copy.start()

    row_ids = lax.broadcasted_iota(jnp.int32, (STATES, STATES), 0)
    col_ids = lax.broadcasted_iota(jnp.int32, (STATES, STATES), 1)

    def rows(j):
        for pair in range(PAIRS):
            same, other = [
                ref[at, :, pair] if whole else ref[at]
                for ref, at, whole in panels[4 * j + 2 * pair : 4 * j + 2 * pair + 2]
            ]
            even = jnp.where(core == 0, same, other)
            odd = jnp.where(core == 0, other, same)
            here = sources[j] * PAIRS + pair
            valid = (row_ids < sizes[0, here]) & (col_ids < sizes[1, here])
            x_high[j, pair], x_low[j, pair] = split(jnp.where(valid, interleave(even, odd), 0.0))

    for j in range(AHEAD):
        fetch(j)
    total[...] = before[...] if last else jnp.zeros(SUMS, F32)
    for j in range(len(parts)):
        rows(j)
    for j, source in enumerate(sources):
        if j + AHEAD < len(parts):
            fetch(j + AHEAD)
        for copy in env(j):
            copy.wait()
        inner = []
        for slot in range(SLOTS):
            pair = codes[0, slot, 0, source] // 2
            x = x_high[j, pair], x_low[j, pair]
            product = dot3(split(lefts[j, slot]), x, ((1,), (0,)))
            inner.append(split(product * scales[0, slot, 0, source]))
        for slot in range(SLOTS):
            target = codes[0, slot, 0, source] % 2
            total[target] += dot3(inner[slot], split(rights[j, slot]), ((1,), (1,)))
    if last:
        for pair in range(PAIRS):
            pairs = total[pair].reshape(RUNS, 2, ROWS, STATES)
            keep[:, pair] = jnp.where(core == 0, pairs[:, 0], pairs[:, 1])
            give[:, pair] = jnp.where(core == 0, pairs[:, 1], pairs[:, 0])


def chunk(parts, lists, panels, left, right, before):
    last = before is not None
    count = len(parts)
    smem, vmem, hbm = (
        pl.BlockSpec(memory_space=space) for space in (pltpu.SMEM, pltpu.VMEM, pl.ANY)
    )
    arrays = []
    for array, *_ in panels:
        if not any(array is known for known in arrays):
            arrays.append(array)
    at = [[array is known for known in arrays].index(True) for array, *_ in panels]

    def kernel(*refs):
        here = [(refs[3 + k], *panel[1:]) for k, panel in zip(at, panels)]
        chunk_kernel(parts, last, *refs[:3], *here, *refs[3 + len(arrays) :])

    result = pl.pallas_call(
        kernel,
        in_specs=[smem] * 3 + [vmem] * len(arrays) + [hbm] * 2 + [vmem] * last,
        out_specs=[vmem] * (2 if last else 1),
        out_shape=[jax.ShapeDtypeStruct(HALF, F32)] * 2
        if last
        else [jax.ShapeDtypeStruct(SUMS, F32)],
        scratch_shapes=[pltpu.VMEM(SUMS, F32)] * last
        + [
            pltpu.VMEM((count,) + SUMS, BF16),
            pltpu.VMEM((count,) + SUMS, BF16),
            pltpu.VMEM((count, SLOTS, STATES, STATES), F32),
            pltpu.VMEM((count, SLOTS, STATES, STATES), F32),
            pltpu.SemaphoreType.DMA((count, 2)),
        ],
        cost_estimate=pl.CostEstimate(flops=LONG if last else 10**9, bytes_accessed=2**20, transcendentals=0),
        compiler_params=pltpu.CompilerParams(vmem_limit_bytes=LIMIT),
    )(*lists, *arrays, left, right, *([before] if last else []))
    return result if last else result[0]


def swap_core(value):
    return lax.ppermute(value, "core", [(0, 1), (1, 0)])


def ahead(value, step):
    return lax.ppermute(value, "x", [(x, (x + step) % 4) for x in range(4)])


def across(value):
    return lax.ppermute(value, "y_hi", [(0, 1), (1, 0)])


def local(
    wavefunction, sector_sizes, env_left, env_right, mpo_weight, bond_index, in_pair, out_pair
):
    core = lax.axis_index("core")
    my_y, my_x = lax.axis_index("y_hi"), lax.axis_index("x")
    left, right = env_left[0, 0], env_right[0, 0]

    runs = lax.all_to_all(
        jnp.broadcast_to(wavefunction[None], (RUNS,) + wavefunction.shape), ("y_lo", "z"), 0, 0
    )
    runs = runs[None]
    (crossed, *beside), (bond_index, in_pair, out_pair, sizes) = lax.optimization_barrier(
        (
            [across(runs), *[ahead(runs, step) for step in STEPS[1:3]]],
            (bond_index, in_pair, out_pair, sector_sizes),
        )
    )
    live = out_pair >= 0
    picked = bond_index[..., None] == jnp.arange(mpo_weight.shape[0], dtype=jnp.int32)
    scales = jnp.where(live, jnp.sum(jnp.where(picked, mpo_weight, 0.0), axis=-1), 0.0)
    codes = in_pair * 2 + jnp.maximum(out_pair, 0)
    lists = (
        jnp.minimum(sizes.T, STATES),
        *[lax.transpose(array, (0, 3, 1, 2)) for array in (codes, scales)],
    )
    column, row = jnp.concatenate([runs, crossed]), jnp.concatenate(beside)
    far_row, far_column = across(row), ahead(column, STEPS[3])

    near = [runs, crossed, *beside]
    panels = []
    for piece in near:
        other = swap_core(piece)
        panels += [(array, 0, True) for array in (piece, other)] * 2
    sums = chunk([(0, 0), (1, 0), (0, 1), (0, 2)], lists, panels, left, right, None)

    far_row, far_column, sums = lax.optimization_barrier((far_row, far_column, sums))
    row, column = (far_row, swap_core(far_row)), (far_column, swap_core(far_column))
    places = [(row, 0), (row, 1), (column, 0), (column, 1)]
    panels = [(array, at, True) for held, at in places for array in held * 2]
    parts = [(1, 1), (1, 2), (0, 3), (1, 3)]
    keep, give = chunk(parts, lists, panels, left, right, sums)
    half = keep + swap_core(give)
    summed = lax.all_to_all(half, ("y_lo", "z"), 0, 0).sum(0)

    owner = (lax.axis_index("y_lo") * 8 + lax.axis_index("z")) * 2 + core
    group_sizes = lax.dynamic_slice_in_dim(sector_sizes, (my_y * 4 + my_x) * PAIRS, PAIRS, 0)
    row_ids = owner * ROWS + jnp.arange(ROWS, dtype=jnp.int32)
    col_ids = jnp.arange(STATES, dtype=jnp.int32)
    valid = (row_ids[None, :, None] < group_sizes[:, 0, None, None]) & (
        col_ids[None, None, :] < group_sizes[:, 1, None, None]
    )
    return jnp.where(valid, summed, 0.0)


def solution(mesh):
    fine = Mesh(mesh.devices.reshape(2, 4, 2, 8, 2), ("y_hi", "x", "y_lo", "z", "core"))
    blk, sec = ("y_hi", "x"), ("y_lo", "z", "core")
    return jax.shard_map(
        local,
        mesh=fine,
        in_specs=(
            P(blk, sec, None),
            P(),
            P(blk, sec, None, None, None, None),
            P(blk, sec, None, None, None, None),
            P(),
            P(blk, sec, None, None),
            P(blk, sec, None, None),
            P(blk, sec, None, None),
        ),
        out_specs=P(blk, sec, None),
        check_vma=False,
    )
```
